1024 devices in a mesh: expert: 64 (over z, core), tensor: 16 (over y, x).
Axes of the slice: x: 4, y: 4, z: 32, core: 2. Of those that a mesh axis runs over, the one named last changes fastest.
Arguments:
- tokens: bfloat16 [8192, 5120], P('expert'), may hold values from -6 to 6
- cotangent: bfloat16 [8192, 5120], P('expert'), may hold values from -6 to 6
- route_devices: int32 [8192, 3], P('expert'), may hold values from 0 to 63, all different within a row; in each aligned block of 128 rows (0 to 127, 128 to 255, ...) at most 7 rows name the same one
- gate_fixed: int32 [8192, 6], P('expert'), may hold values from 4096 to 65535
- w_gate: bfloat16 [128, 768, 5120], P('expert', 'tensor'), may hold values from -0.125 to 0.125
- w_up: bfloat16 [128, 768, 5120], P('expert', 'tensor'), may hold values from -0.078125 to 0.078125
- w_down: bfloat16 [128, 768, 5120], P('expert', 'tensor'), may hold values from -0.3125 to 0.3125
Outputs:
- mixed: bfloat16 [8192, 5120], P('expert', 'tensor')
- token_grad: bfloat16 [8192, 5120], P('expert', 'tensor')
The draws below stay inside these ranges and needn't reach their ends.
Inputs may be any that keep to these rules, and one draw needn't show every extreme that they name: `route_devices`: each row names 3 different devices. Among the tokens of one expert index no device is named by more than 7 of them, and some device is named by exactly 7 in some blocks.
All inputs are finite; a program needn't handle non-finite values.
Results may differ from the reference program's by a relative error of at most 0.02.
Values may be sent and summed in bfloat16 or wider, within the bound.
No kernel may reach another device: no remote copies, remote signals or barrier semaphores. Data moves between devices by JAX's collectives and lax.ppermute only.
A program may use at most 64 MiB of HBM per device.

```python
import math
import jax
import jax.numpy as jnp
import numpy as np
from jax import lax

D = 5120
FF = 768
EXP_DEV = 2
ROUTE_DEVS = 3
TOK_DEV = 128
EXPERTS = 128
TOKENS = 8192
CAP = 7
N_EXPERT = 64
N_TENSOR = 16


def plant(drawn, key, smallest, high):
    extent = drawn.shape
    place = [jax.random.randint(jax.random.fold_in(key, axis), (), 0, extent[axis]) for axis in range(len(extent))]
    drawn = drawn.at[tuple(place)].set(smallest)
    longest = extent.index(max(extent))
    place[longest] = (place[longest] + 1) % extent[longest]
    return drawn.at[tuple(place)].set(high)


def strengthened(drawn, key, source, target, blocks, factor):
    owner, partner = [(jnp.arange(drawn.shape[axis_at]) // (drawn.shape[axis_at] // blocks)).reshape([-1 if axis == axis_at else 1 for axis in range(drawn.ndim)]) for axis_at in (source, target)]
    chosen = jax.random.permutation(key, blocks)[partner]
    strong = (owner == chosen) | (owner == (partner + blocks // 2) % blocks)
    return jnp.where(strong, factor * drawn, drawn)


def block_scale(own_key, dims, split, least, high):
    gain = 1.0
    for axis_at, shards_of in split:
        draws = jax.random.uniform(jax.random.fold_in(jax.random.fold_in(own_key, 6), axis_at), (shards_of,), jnp.float32, least / len(split), high / len(split))
        gain = gain * jnp.repeat(jnp.exp(draws), dims[axis_at] // shards_of).reshape((-1,) + (1,) * (len(dims) - 1 - axis_at))
    return gain


def assign_block(rng, own, number, rows, amount, top, most, skew):
    ranking = jax.random.permutation(rng, amount)
    heavy_load, common = load_shares(amount, rows * top, most, skew, True), load_shares(amount, rows * top, most, skew, False)
    places = jnp.arange(amount)

    def named(sizes, offset_by):
        used = int((sizes > 0).sum())
        fixed = max(1, used // 4)
        moved = fixed + (places - fixed + offset_by * (used - fixed)) % max(1, amount - fixed)
        return jnp.zeros((amount,), jnp.int32).at[ranking[jnp.where(places < fixed, places, moved)]].set(jnp.asarray(sizes, jnp.int32))

    sizes = jnp.where(number % 4 == 0, named(heavy_load, number // 4), named(common, number - number // 4 - 1))
    mixed = jax.random.permutation(jax.random.fold_in(own, 3), amount)
    donor, taker = mixed[0:amount // 2 * 2:2], mixed[1:amount // 2 * 2:2]
    slack = jnp.minimum(sizes[donor] - 1, most - sizes[taker]) // 2
    slack = jnp.where((donor == ranking[0]) | (taker == ranking[0]) | (sizes[taker] == 0), 0, jnp.maximum(slack, 0))
    moved = jax.random.randint(jax.random.fold_in(own, 4), (amount // 2,), 0, 1 << 20) % (slack + 1)
    sizes = sizes.at[donor].add(-moved).at[taker].add(moved)
    labels = jnp.searchsorted(jnp.cumsum(sizes), jnp.arange(rows * top), side="right").astype(jnp.int32)
    grid = labels.reshape(top, rows).T
    grid = grid[jax.random.permutation(jax.random.fold_in(own, 1), rows)]
    offset_by = jax.random.randint(jax.random.fold_in(own, 2), (rows, 1), 0, top)
    return jnp.take_along_axis(grid, (jnp.arange(top)[None, :] + offset_by) % top, axis=1)


def load_shares(count, total, bound, skew, full):
    weights = [(1 << 20) // math.isqrt(standing ** skew) + 1 for standing in range(1, count + 1)]
    largest = bound if full else min(bound, max(-(-total // count), total * weights[0] // sum(weights)))
    least = 1 if total - largest >= count - 1 else 0
    counts, spare = [largest] + [least] * (count - 1), total - largest - least * (count - 1)
    while spare > 0:
        movable = [i for i in range(1, count) if counts[i] < largest] or [i for i in range(1, count) if counts[i] < bound]
        mass, budget = sum([weights[i] for i in movable]), spare
        for i in movable:
            addition = min(bound - counts[i], max(1, budget * weights[i] // mass), spare)
            counts[i] = counts[i] + addition
            spare = spare - addition
    return np.array(counts)


def normal_values(stream_key, extent, scale, limit, cuts=(), kind=jnp.bfloat16):
    drawn = jax.random.normal(stream_key, extent, jnp.float32) * scale
    if len(cuts) > 0:
        drawn = block_scale(stream_key, extent, cuts, -0.22, 0.18) * drawn
    return jnp.clip(drawn, min=-limit, max=limit).astype(kind)


def noise_with(rng, dims, deviation, bound, cuts, heavy, held_as=jnp.bfloat16):
    values = deviation * jax.random.normal(rng, dims, jnp.float32)
    if cuts:
        values = values * block_scale(rng, dims, cuts, -0.22, 0.18)
    return jnp.clip(strengthened(values, jax.random.fold_in(rng, 3), *heavy), -bound, bound).astype(held_as)


def setup_inputs(seed: int = 0) -> dict:
    key_list = jax.random.split(jax.random.key(seed), 8)
    tokens = normal_values(key_list[0], (TOKENS, D), 1.0, 6.0, ((0, 64),))
    cotangent = normal_values(key_list[1], (TOKENS, D), 1.0, 6.0, ((0, 64),))
    route_devices_keys = jax.random.split(jax.random.fold_in(key_list[2], 1), TOKENS // TOK_DEV)
    route_devices_turns = jax.random.permutation(jax.random.fold_in(key_list[2], 3), TOKENS // TOK_DEV)
    route_devices = jax.vmap(lambda own, number: assign_block(jax.random.fold_in(key_list[2], 2), own, number, TOK_DEV, N_EXPERT, ROUTE_DEVS, CAP, 2))(route_devices_keys, route_devices_turns).reshape((TOKENS, ROUTE_DEVS))
    gate_fixed = plant(jax.random.randint(key_list[3], (TOKENS, ROUTE_DEVS * EXP_DEV), 4096, 65536), jax.random.fold_in(key_list[3], 1), 4096, 65535).astype(jnp.int32)
    w_gate = noise_with(key_list[4], (EXPERTS, FF, D), D ** -0.5, 0.125, ((0, 64), (1, 16)), (1, 2, 16, 2.0))
    w_up = normal_values(key_list[5], (EXPERTS, FF, D), D ** -0.5, 0.078125, ((0, 64), (1, 16)))
    w_down = noise_with(key_list[6], (EXPERTS, FF, D), FF ** -0.5, 0.3125, ((0, 64), (1, 16)), (1, 2, 16, 2.0))
    return {"tokens": tokens, "cotangent": cotangent, "route_devices": route_devices, "gate_fixed": gate_fixed, "w_gate": w_gate, "w_up": w_up, "w_down": w_down}


def to_half(values):
    return lax.optimization_barrier(values.astype(jnp.bfloat16))


def silu_parts(pre_gate):
    sigma = jax.nn.sigmoid(pre_gate)
    return pre_gate * sigma, sigma * (1.0 + pre_gate * (1.0 - sigma))


def slot_table(route_devices):
    blocks = route_devices.reshape(N_EXPERT, TOK_DEV * ROUTE_DEVS)
    devices = jnp.arange(N_EXPERT, dtype=jnp.int32)

    def one_block(dests):
        onehot = (dests[:, None] == devices[None, :]).astype(jnp.int32)
        prior = jnp.cumsum(onehot, axis=0) - onehot
        return jnp.sum(prior * onehot, axis=1).astype(jnp.int32)

    return jax.vmap(one_block)(blocks).reshape(TOKENS, ROUTE_DEVS)


def reference(tokens, cotangent, route_devices, gate_fixed, w_gate, w_up, w_down):
    width = N_EXPERT * CAP
    split_hidden = FF // N_TENSOR
    slots = slot_table(route_devices)
    source = (jnp.arange(TOKENS, dtype=jnp.int32) // TOK_DEV)[:, None]
    rows = (source * CAP + slots).astype(jnp.int32)
    gates = (gate_fixed.astype(jnp.float32) / 65536.0).astype(jnp.bfloat16)
    gates = gates.reshape(TOKENS, ROUTE_DEVS, EXP_DEV)
    token_copies = jnp.broadcast_to(tokens[:, None, :], (TOKENS, ROUTE_DEVS, D))
    cot_copies = jnp.broadcast_to(cotangent[:, None, :], (TOKENS, ROUTE_DEVS, D))
    token_buf = jnp.zeros((N_EXPERT, width, D), jnp.bfloat16).at[route_devices, rows].set(token_copies)
    cot_buf = jnp.zeros((N_EXPERT, width, D), jnp.bfloat16).at[route_devices, rows].set(cot_copies)
    gate_buf = jnp.zeros((N_EXPERT, width, EXP_DEV), jnp.bfloat16).at[route_devices, rows].set(gates)
    gate_w = w_gate.reshape(N_EXPERT, EXP_DEV, FF, D)
    up_w = w_up.reshape(N_EXPERT, EXP_DEV, FF, D)
    down_w = w_down.reshape(N_EXPERT, EXP_DEV, FF, D)

    def one_device(items):
        rows_in, cot_in, gates_in, gate_mat, up_mat, down_mat = items
        rows32 = rows_in.astype(jnp.float32)
        cot32 = cot_in.astype(jnp.float32)
        gate32 = gate_mat.astype(jnp.float32)
        up32 = up_mat.astype(jnp.float32)
        down32 = down_mat.astype(jnp.float32)
        scale = gates_in.astype(jnp.float32).T
        pre_gate = jnp.einsum("rd,efd->erf", rows32, gate32)
        pre_up = jnp.einsum("rd,efd->erf", rows32, up32)
        activated, slope = silu_parts(pre_gate)
        hidden = to_half(activated * pre_up * scale[:, :, None]).astype(jnp.float32)
        hidden4 = hidden.reshape(EXP_DEV, width, N_TENSOR, split_hidden)
        down4 = down32.reshape(EXP_DEV, N_TENSOR, split_hidden, D)
        parts = jnp.einsum("erqh,eqhd->qrd", hidden4, down4)
        out_row = jnp.sum(to_half(parts).astype(jnp.float32), axis=0).astype(jnp.bfloat16)
        back_hidden = jnp.einsum("rd,efd->erf", cot32, down32) * scale[:, :, None]
        grad_gate = to_half(back_hidden * pre_up * slope).astype(jnp.float32)
        grad_up = to_half(back_hidden * activated).astype(jnp.float32)
        grad_gate4 = grad_gate.reshape(EXP_DEV, width, N_TENSOR, split_hidden)
        grad_up4 = grad_up.reshape(EXP_DEV, width, N_TENSOR, split_hidden)
        gate4 = gate32.reshape(EXP_DEV, N_TENSOR, split_hidden, D)
        up4 = up32.reshape(EXP_DEV, N_TENSOR, split_hidden, D)
        grad_parts = jnp.einsum("erqh,eqhd->qrd", grad_gate4, gate4) + jnp.einsum("erqh,eqhd->qrd", grad_up4, up4)
        grad_row = jnp.sum(to_half(grad_parts).astype(jnp.float32), axis=0).astype(jnp.bfloat16)
        return out_row, grad_row

    out_buf, grad_buf = lax.map(one_device, (token_buf, cot_buf, gate_buf, gate_w, up_w, down_w))
    mixed = jnp.sum(out_buf[route_devices, rows].astype(jnp.float32), axis=1).astype(jnp.bfloat16)
    token_grad = jnp.sum(grad_buf[route_devices, rows].astype(jnp.float32), axis=1).astype(jnp.bfloat16)
    return mixed, token_grad
```

```python
import jax
import jax.numpy as jnp
from jax import lax
from jax.sharding import Mesh
from jax.sharding import PartitionSpec as P

BF16 = jnp.bfloat16
F32 = jnp.float32
ROWS = 8
LANES = 128


def ring(size, step):
    return [(i, (i + step) % size) for i in range(size)]


def routing(named, gate, core, n_z):
    fanout, count = named.shape
    dests = 2 * lax.broadcasted_iota(jnp.int32, (n_z, count), 0) + core
    hits = [named[k][None, :] == dests for k in range(fanout)]
    member = hits[0]
    for hit in hits[1:]:
        member = member | hit
    earlier = (
        lax.broadcasted_iota(jnp.int32, (count, count), 0)
        < lax.broadcasted_iota(jnp.int32, (count, count), 1)
    ).astype(BF16)
    prior = jnp.dot(member.astype(BF16), earlier, preferred_element_type=F32).astype(jnp.int32)
    slot = jnp.where(member, prior, -1)
    chosen = slot[:, None, :] == lax.broadcasted_iota(jnp.int32, (n_z, ROWS, count), 1)
    gate_row = []
    for e in range(2):
        value = jnp.zeros((n_z, count), F32)
        for k in range(fanout):
            value = value + jnp.where(hits[k], gate[2 * k + e][None, :].astype(F32), 0.0)
        gate_row.append(jnp.sum(jnp.where(chosen, value[:, None, :], 0.0), axis=2))
    return (
        chosen.astype(BF16).reshape(n_z * ROWS, count),
        jnp.concatenate(gate_row, axis=1).astype(BF16),
    )


def per_device(tokens, cotangent, route_devices, gate_fixed, w_gate, w_up, w_down):
    n_z = lax.axis_size("z")
    n_y, n_x = lax.axis_size("y"), lax.axis_size("x")
    core, y, x = lax.axis_index("c"), lax.axis_index("y"), lax.axis_index("x")
    count, width = tokens.shape
    fanout = route_devices.shape[1]
    local_experts, units, _ = w_gate.shape
    group = local_experts * units
    quarter = width // n_y
    part_width = quarter // 2
    rows = n_z * ROWS

    kinds = jnp.concatenate([w.reshape(group, width) for w in (w_gate, w_up, w_down)], axis=0)
    blocks = []
    for d in range(n_y):
        block = lax.dynamic_slice_in_dim(kinds, ((y + d) % n_y) * quarter, quarter, 1)
        blocks.append(block if d == 0 else lax.ppermute(block, "y", ring(n_y, d)))
    padded = [
        jnp.pad(b.reshape(3, group, quarter), ((0, 0), (0, LANES - group), (0, 0))) for b in blocks
    ]
    w_in = jnp.concatenate([p[:2].reshape(2 * LANES, quarter) for p in padded], axis=0)
    w_back = jnp.concatenate([p[2] for p in padded], axis=0)
    chunk = quarter // n_x
    mix = []
    for j in range(n_x):
        top = jnp.pad(w_back[:, j * chunk : (j + 1) * chunk], ((0, 0), (0, chunk)))
        low = jnp.pad(w_in[:, j * chunk : (j + 1) * chunk], ((0, 0), (chunk, 0)))
        mix.append(jnp.concatenate([top, low], axis=0))
    w_out = jnp.concatenate(mix, axis=1)

    offset = quarter * y + part_width * (x % 2)
    part = jnp.where(
        x < 2,
        lax.dynamic_slice_in_dim(tokens, offset, part_width, 1),
        lax.dynamic_slice_in_dim(cotangent, offset, part_width, 1),
    )
    gate = (gate_fixed.astype(F32) / 65536.0).astype(BF16).T
    aux = jnp.concatenate([route_devices.T.astype(BF16), gate], axis=0)
    aux = jnp.pad(aux, ((0, 16 - aux.shape[0]), (0, part_width - count)))
    both = lax.ppermute(jnp.concatenate([part, aux], axis=0), "c", [(0, 1), (1, 0)])
    other_part, other_aux = both[:count], both[count:, :count]
    other_named = other_aux[:fanout].astype(jnp.int32)
    halves = [
        (other_part, *routing(other_named, other_aux[fanout : 3 * fanout], core, n_z)),
        (part, *routing(route_devices.T, gate, core, n_z)),
    ]

    def dispatch(part, onehot, gate_row):
        sent = jnp.dot(onehot, part, preferred_element_type=BF16).reshape(n_z, ROWS, part_width)
        last = jnp.pad(gate_row, ((0, 0), (0, part_width - gate_row.shape[1])))[:, None, :]
        is_last = lax.broadcasted_iota(jnp.int32, sent.shape, 1) == ROWS - 1
        sent = jnp.where(is_last, last, sent)
        return lax.all_to_all(sent, "z", split_axis=0, concat_axis=0, tiled=True)

    def experts(received):
        flat = received.reshape(rows, part_width)
        owner = lax.broadcasted_iota(jnp.int32, (rows, n_z), 0) // ROWS
        spread = (owner == lax.broadcasted_iota(jnp.int32, (rows, n_z), 1)).astype(BF16)
        spread = jnp.dot(spread, received[:, ROWS - 1, :LANES], preferred_element_type=F32)
        lane = lax.broadcasted_iota(jnp.int32, (rows, LANES), 1)
        mine = lax.broadcasted_iota(jnp.int32, (rows, LANES), 0) % ROWS
        columns = [
            jnp.sum(jnp.where(lane == e * ROWS + mine, spread, 0.0), axis=1, keepdims=True)
            for e in range(local_experts)
        ]
        scale = jnp.where(lane < units, columns[0], columns[1])

        pieces = [flat] + [lax.ppermute(flat, "x", ring(n_x, d)) for d in range(1, n_x)]
        stack = jnp.stack(pieces)

        def piece(j):
            return lax.dynamic_index_in_dim(stack, (x - j) % n_x, 0, keepdims=False)

        tok_rows = jnp.concatenate([piece(0), piece(1)], axis=1)
        cot_rows = jnp.concatenate([piece(2), piece(3)], axis=1)
        contract = (((1,), (1,)), ((), ()))
        pre = lax.dot_general(tok_rows, w_in, contract, preferred_element_type=F32)
        back = lax.dot_general(cot_rows, w_back, contract, preferred_element_type=F32)
        total = None
        for d in range(n_y):
            term = jnp.concatenate(
                [pre[:, 2 * LANES * d : 2 * LANES * (d + 1)], back[:, LANES * d : LANES * (d + 1)]],
                axis=1,
            )
            if d > 0:
                term = lax.ppermute(term.astype(BF16), "y", ring(n_y, -d)).astype(F32)
            total = term if total is None else total + term
        pre_gate, pre_up = total[:, :LANES], total[:, LANES : 2 * LANES]
        back_hidden = total[:, 2 * LANES :] * scale
        sigma = jax.nn.sigmoid(pre_gate)
        activated = pre_gate * sigma
        slope = sigma * (1.0 + pre_gate * (1.0 - sigma))
        hidden = (activated * pre_up * scale).astype(BF16)
        grad_gate = (back_hidden * pre_up * slope).astype(BF16)
        grad_up = (back_hidden * activated).astype(BF16)
        terms = jnp.concatenate([hidden, grad_gate, grad_up], axis=1)
        gathered = [terms] + [lax.ppermute(terms, "y", ring(n_y, d)) for d in range(1, n_y)]
        left = jnp.concatenate(
            [g[:, :LANES] for g in gathered] + [g[:, LANES:] for g in gathered], axis=1
        )
        out = jnp.dot(left, w_out, preferred_element_type=F32).astype(BF16)
        summed = None
        for d in range(n_x):
            block = lax.dynamic_slice_in_dim(out, ((x + d) % n_x) * part_width, part_width, 1)
            if d > 0:
                block = lax.ppermute(block, "x", ring(n_x, d))
            summed = block.astype(F32) if summed is None else summed + block.astype(F32)
        return summed.astype(BF16).reshape(n_z, ROWS, part_width)

    def give_back(back_rows):
        return lax.all_to_all(back_rows, "z", split_axis=0, concat_axis=0, tiled=True)

    def combine(onehot, returned):
        return lax.dot_general(
            onehot,
            returned.reshape(rows, part_width),
            (((0,), (0,)), ((), ())),
            preferred_element_type=F32,
        )

    arrived = [dispatch(*half) for half in halves]
    first = experts(arrived[0])
    first, second = lax.optimization_barrier((first, arrived[1]))
    returned = [give_back(first), give_back(experts(second))]
    theirs = combine(halves[0][1], returned[0]).astype(BF16)
    theirs = lax.ppermute(theirs, "c", [(0, 1), (1, 0)])
    result = (combine(halves[1][1], returned[1]) + theirs.astype(F32)).astype(BF16)
    return result[:, :chunk], result[:, chunk:]


def solution(mesh):
    n_expert, n_tensor = mesh.devices.shape
    fine = Mesh(mesh.devices.reshape(n_expert // 2, 2, 4, n_tensor // 4), ("z", "c", "y", "x"))
    tokens = P(("z", "c"), None)
    weights = P(("z", "c"), ("y", "x"), None)
    outs = P(("z", "c"), ("y", "x"))
    return jax.shard_map(
        per_device,
        mesh=fine,
        in_specs=(tokens, tokens, tokens, tokens, weights, weights, weights),
        out_specs=(outs, outs),
        check_vma=False,
    )
```

```python
import jax
import jax.numpy as jnp
from jax import lax
from jax.sharding import Mesh
from jax.sharding import PartitionSpec as P

BF16 = jnp.bfloat16
F32 = jnp.float32
ROWS = 8
LANES = 128


def ring(size, step):
    return [(i, (i + step) % size) for i in range(size)]


def routing(named, gate, core, n_z):
    fanout, count = named.shape
    dests = 2 * lax.broadcasted_iota(jnp.int32, (n_z, count), 0) + core
    hits = [named[k][None, :] == dests for k in range(fanout)]
    member = hits[0]
    for hit in hits[1:]:
        member = member | hit
    earlier = (
        lax.broadcasted_iota(jnp.int32, (count, count), 0)
        < lax.broadcasted_iota(jnp.int32, (count, count), 1)
    ).astype(BF16)
    prior = jnp.dot(member.astype(BF16), earlier, preferred_element_type=F32).astype(jnp.int32)
    slot = jnp.where(member, prior, -1)
    chosen = slot[:, None, :] == lax.broadcasted_iota(jnp.int32, (n_z, ROWS, count), 1)
    gate_row = []
    for e in range(2):
        value = jnp.zeros((n_z, count), F32)
        for k in range(fanout):
            value = value + jnp.where(hits[k], gate[2 * k + e][None, :].astype(F32), 0.0)
        gate_row.append(jnp.sum(jnp.where(chosen, value[:, None, :], 0.0), axis=2))
    return (
        chosen.astype(BF16).reshape(n_z * ROWS, count),
        jnp.concatenate(gate_row, axis=1).astype(BF16),
    )


def exchange_weights(kinds, axis, n_groups, group, quarter):
    place = lax.axis_index(axis)
    blocks = []
    for d in range(n_groups):
        block = lax.dynamic_slice_in_dim(kinds, ((place + d) % n_groups) * quarter, quarter, 1)
        blocks.append(block if d == 0 else lax.ppermute(block, axis, ring(n_groups, d)))
    padded = [
        jnp.pad(b.reshape(3, group, quarter), ((0, 0), (0, LANES - group), (0, 0))) for b in blocks
    ]
    w_in = jnp.concatenate([p[:2].reshape(2 * LANES, quarter) for p in padded], axis=0)
    w_back = jnp.concatenate([p[2] for p in padded], axis=0)
    return w_in, w_back


def feature_part(tokens, cotangent, major, minor, quarter):
    half = quarter // 2
    offset = quarter * major + half * (minor % 2)
    return jnp.where(
        minor < 2,
        lax.dynamic_slice_in_dim(tokens, offset, half, 1),
        lax.dynamic_slice_in_dim(cotangent, offset, half, 1),
    )


def gate_scale(received, units):
    n_z = received.shape[0]
    rows = n_z * ROWS
    owner = lax.broadcasted_iota(jnp.int32, (rows, n_z), 0) // ROWS
    spread = (owner == lax.broadcasted_iota(jnp.int32, (rows, n_z), 1)).astype(BF16)
    spread = jnp.dot(spread, received[:, ROWS - 1, :LANES], preferred_element_type=F32)
    lane = lax.broadcasted_iota(jnp.int32, (rows, LANES), 1)
    mine = lax.broadcasted_iota(jnp.int32, (rows, LANES), 0) % ROWS
    columns = [
        jnp.sum(jnp.where(lane == e * ROWS + mine, spread, 0.0), axis=1, keepdims=True)
        for e in range(2)
    ]
    return jnp.where(lane < units, columns[0], columns[1])


def experts(received, w_in, w_back, major, minor, units):
    n_major, n_minor = lax.axis_size(major), lax.axis_size(minor)
    place = lax.axis_index(minor)
    n_z, _, half = received.shape
    rows = n_z * ROWS
    flat = received.reshape(rows, half)
    stack = jnp.stack([flat] + [lax.ppermute(flat, minor, ring(n_minor, d)) for d in range(1, n_minor)])
    scale = gate_scale(received, units)

    def piece(j):
        return lax.dynamic_index_in_dim(stack, (place - j) % n_minor, 0, keepdims=False)

    tok_rows = jnp.concatenate([piece(0), piece(1)], axis=1)
    cot_rows = jnp.concatenate([piece(2), piece(3)], axis=1)
    contract = (((1,), (1,)), ((), ()))
    pre = lax.dot_general(tok_rows, w_in, contract, preferred_element_type=F32)
    back = lax.dot_general(cot_rows, w_back, contract, preferred_element_type=F32)
    total = None
    for d in range(n_major):
        term = jnp.concatenate(
            [pre[:, 2 * LANES * d : 2 * LANES * (d + 1)], back[:, LANES * d : LANES * (d + 1)]],
            axis=1,
        )
        if d > 0:
            term = lax.ppermute(term.astype(BF16), major, ring(n_major, -d)).astype(F32)
        total = term if total is None else total + term
    pre_gate, pre_up = total[:, :LANES], total[:, LANES : 2 * LANES]
    back_hidden = total[:, 2 * LANES :] * scale
    sigma = jax.nn.sigmoid(pre_gate)
    activated = pre_gate * sigma
    slope = sigma * (1.0 + pre_gate * (1.0 - sigma))
    hidden = (activated * pre_up * scale).astype(BF16)
    grad_gate = (back_hidden * pre_up * slope).astype(BF16)
    grad_up = (back_hidden * activated).astype(BF16)
    terms = jnp.concatenate([hidden, grad_gate, grad_up], axis=1)
    gathered = [terms] + [lax.ppermute(terms, major, ring(n_major, d)) for d in range(1, n_major)]
    hidden_all = jnp.concatenate([g[:, :LANES] for g in gathered], axis=1)
    grads_all = jnp.concatenate([g[:, LANES:] for g in gathered], axis=1)
    out = jnp.dot(hidden_all, w_back, preferred_element_type=F32).astype(BF16)
    grad = jnp.dot(grads_all, w_in, preferred_element_type=F32).astype(BF16)
    chunk = half // 2
    blocks = jnp.stack(
        [
            jnp.concatenate(
                [out[:, j * chunk : (j + 1) * chunk], grad[:, j * chunk : (j + 1) * chunk]], axis=1
            )
            for j in range(n_minor)
        ]
    )
    summed = None
    for d in range(n_minor):
        block = lax.dynamic_index_in_dim(blocks, (place + d) % n_minor, 0, keepdims=False)
        if d > 0:
            block = lax.ppermute(block, minor, ring(n_minor, d))
        summed = block.astype(F32) if summed is None else summed + block.astype(F32)
    return summed.astype(BF16).reshape(n_z, ROWS, half)


def per_device(tokens, cotangent, route_devices, gate_fixed, w_gate, w_up, w_down):
    n_z, n_y, n_x = lax.axis_size("z"), lax.axis_size("y"), lax.axis_size("x")
    core, y, x = lax.axis_index("c"), lax.axis_index("y"), lax.axis_index("x")
    count, width = tokens.shape
    fanout = route_devices.shape[1]
    local_experts, units, _ = w_gate.shape
    group = local_experts * units
    quarter = width // n_y
    half = quarter // 2

    own = feature_part(tokens, cotangent, y, x, quarter)
    gate = (gate_fixed.astype(F32) / 65536.0).astype(BF16).T
    named = route_devices.T
    aux = jnp.concatenate([named.astype(BF16), gate], axis=0)
    aux = jnp.pad(aux, ((0, 16 - aux.shape[0]), (0, half - count)))
    lent = jnp.concatenate([feature_part(tokens, cotangent, x, y, quarter), aux], axis=0)
    other = lax.ppermute(lent, "c", [(0, 1), (1, 0)])
    other_aux = other[count:, :count]
    halves = [
        (own, *routing(named, gate, core, n_z)),
        (
            other[:count],
            *routing(
                other_aux[:fanout].astype(jnp.int32), other_aux[fanout : 3 * fanout], core, n_z
            ),
        ),
    ]

    def dispatch(part, onehot, gate_row):
        sent = jnp.dot(onehot, part, preferred_element_type=BF16).reshape(n_z, ROWS, half)
        last = jnp.pad(gate_row, ((0, 0), (0, half - gate_row.shape[1])))[:, None, :]
        is_last = lax.broadcasted_iota(jnp.int32, sent.shape, 1) == ROWS - 1
        return jnp.where(is_last, last, sent)

    sent = jnp.concatenate([dispatch(*h) for h in halves], axis=1)
    sent, w_gate, w_up, w_down = lax.optimization_barrier((sent, w_gate, w_up, w_down))
    arrived = lax.all_to_all(sent, "z", split_axis=0, concat_axis=0, tiled=True)

    kinds = jnp.concatenate([w.reshape(group, width) for w in (w_gate, w_up, w_down)], axis=0)
    by_y = exchange_weights(kinds, "y", n_y, group, quarter)
    by_x = exchange_weights(kinds, "x", n_x, group, quarter)
    arrived, by_y, by_x = lax.optimization_barrier((arrived, by_y, by_x))

    results = [
        experts(arrived[:, :ROWS], *by_y, "y", "x", units),
        experts(arrived[:, ROWS:], *by_x, "x", "y", units),
    ]
    returned = lax.all_to_all(
        jnp.concatenate(results, axis=1), "z", split_axis=0, concat_axis=0, tiled=True
    )

    def combine(onehot, rows):
        return lax.dot_general(
            onehot,
            rows.reshape(n_z * ROWS, half),
            (((0,), (0,)), ((), ())),
            preferred_element_type=F32,
        )

    theirs = combine(halves[1][1], returned[:, ROWS:]).astype(BF16)
    swap = [
        ((c * n_y + j) * n_x + i, ((1 - c) * n_y + i) * n_x + j)
        for c in range(2)
        for j in range(n_y)
        for i in range(n_x)
    ]
    theirs = lax.ppermute(theirs, ("c", "y", "x"), swap)
    result = (combine(halves[0][1], returned[:, :ROWS]) + theirs.astype(F32)).astype(BF16)
    return result[:, : half // 2], result[:, half // 2 :]


def solution(mesh):
    n_expert, n_tensor = mesh.devices.shape
    fine = Mesh(mesh.devices.reshape(n_expert // 2, 2, 4, n_tensor // 4), ("z", "c", "y", "x"))
    tokens = P(("z", "c"), None)
    weights = P(("z", "c"), ("y", "x"), None)
    outs = P(("z", "c"), ("y", "x"))
    return jax.shard_map(
        per_device,
        mesh=fine,
        in_specs=(tokens, tokens, tokens, tokens, weights, weights, weights),
        out_specs=(outs, outs),
        check_vma=False,
    )
```

```python
import jax
import jax.numpy as jnp
from jax import lax
from jax.sharding import Mesh
from jax.sharding import PartitionSpec as P

BF16 = jnp.bfloat16
F32 = jnp.float32
ROWS = 8
LANES = 128


def ring(size, step):
    return [(i, (i + step) % size) for i in range(size)]


def routing(named, gate, core, n_z):
    fanout, count = named.shape
    dests = 2 * lax.broadcasted_iota(jnp.int32, (n_z, count), 0) + core
    hits = [named[k][None, :] == dests for k in range(fanout)]
    member = hits[0]
    for hit in hits[1:]:
        member = member | hit
    earlier = (
        lax.broadcasted_iota(jnp.int32, (count, count), 0)
        < lax.broadcasted_iota(jnp.int32, (count, count), 1)
    ).astype(BF16)
    prior = jnp.dot(member.astype(BF16), earlier, preferred_element_type=F32).astype(jnp.int32)
    slot = jnp.where(member, prior, -1)
    chosen = slot[:, None, :] == lax.broadcasted_iota(jnp.int32, (n_z, ROWS, count), 1)
    gate_row = []
    for e in range(2):
        value = jnp.zeros((n_z, count), F32)
        for k in range(fanout):
            value = value + jnp.where(hits[k], gate[2 * k + e][None, :].astype(F32), 0.0)
        gate_row.append(jnp.sum(jnp.where(chosen, value[:, None, :], 0.0), axis=2))
    return (
        chosen.astype(BF16).reshape(n_z * ROWS, count),
        jnp.concatenate(gate_row, axis=1).astype(BF16),
    )


def exchange_weights(kinds, axis, n_groups, group, quarter, absolute):
    place = lax.axis_index(axis)
    w_in = jnp.zeros((n_groups, 2, LANES, quarter), BF16)
    w_back = jnp.zeros((n_groups, LANES, quarter), BF16)
    for d in range(n_groups):
        block = lax.dynamic_slice_in_dim(kinds, ((place + d) % n_groups) * quarter, quarter, 1)
        if d > 0:
            block = lax.ppermute(block, axis, ring(n_groups, d))
        block = block.reshape(3, group, quarter)
        at = (place - d) % n_groups if absolute else d
        w_in = lax.dynamic_update_slice(w_in, block[None, :2], (at, 0, 0, 0))
        w_back = lax.dynamic_update_slice(w_back, block[2:], (at, 0, 0))
    return (
        w_in.reshape(n_groups * 2 * LANES, quarter),
        w_back.reshape(n_groups * LANES, quarter),
    )


def feature_part(tokens, cotangent, major, minor, quarter):
    half = quarter // 2
    offset = quarter * major + half * (minor % 2)
    return jnp.where(
        minor < 2,
        lax.dynamic_slice_in_dim(tokens, offset, half, 1),
        lax.dynamic_slice_in_dim(cotangent, offset, half, 1),
    )


def gate_scale(received, units):
    n_z = received.shape[0]
    rows = n_z * ROWS
    owner = lax.broadcasted_iota(jnp.int32, (rows, n_z), 0) // ROWS
    spread = (owner == lax.broadcasted_iota(jnp.int32, (rows, n_z), 1)).astype(BF16)
    spread = jnp.dot(spread, received[:, ROWS - 1, :LANES], preferred_element_type=F32)
    lane = lax.broadcasted_iota(jnp.int32, (rows, LANES), 1)
    mine = lax.broadcasted_iota(jnp.int32, (rows, LANES), 0) % ROWS
    columns = [
        jnp.sum(jnp.where(lane == e * ROWS + mine, spread, 0.0), axis=1, keepdims=True)
        for e in range(2)
    ]
    return jnp.where(lane < units, columns[0], columns[1])


def swap_blocks(blocks, axis):
    return lax.all_to_all(blocks, axis, split_axis=0, concat_axis=0, tiled=True)


def gather_absolute(value, axis, direct):
    size, place = lax.axis_size(axis), lax.axis_index(axis)
    if direct:
        return swap_blocks(jnp.broadcast_to(value[None], (size, *value.shape)), axis)
    stack = jnp.stack([value] + [lax.ppermute(value, axis, ring(size, d)) for d in range(1, size)])
    return [
        lax.dynamic_index_in_dim(stack, (place - j) % size, 0, keepdims=False) for j in range(size)
    ]


def sum_blocks(blocks, axis, direct):
    size, place = lax.axis_size(axis), lax.axis_index(axis)
    if direct:
        return jnp.sum(swap_blocks(jnp.stack(blocks), axis).astype(F32), axis=0)
    stack = jnp.stack(blocks)
    total = None
    for d in range(size):
        block = lax.dynamic_index_in_dim(stack, (place + d) % size, 0, keepdims=False)
        if d > 0:
            block = lax.ppermute(block, axis, ring(size, d))
        total = block.astype(F32) if total is None else total + block.astype(F32)
    return total


def experts(received, w_in, w_back, major, minor, units, direct):
    n_major, n_minor = lax.axis_size(major), lax.axis_size(minor)
    n_z, _, half = received.shape
    rows = n_z * ROWS
    pieces = gather_absolute(received.reshape(rows, half), minor, direct)
    scale = gate_scale(received, units)
    tok_rows = jnp.concatenate([pieces[0], pieces[1]], axis=1)
    cot_rows = jnp.concatenate([pieces[2], pieces[3]], axis=1)
    contract = (((1,), (1,)), ((), ()))
    pre = lax.dot_general(tok_rows, w_in, contract, preferred_element_type=F32)
    back = lax.dot_general(cot_rows, w_back, contract, preferred_element_type=F32)
    terms = [
        jnp.concatenate(
            [pre[:, 2 * LANES * d : 2 * LANES * (d + 1)], back[:, LANES * d : LANES * (d + 1)]],
            axis=1,
        )
        for d in range(n_major)
    ]
    if direct:
        total = sum_blocks([t.astype(BF16) for t in terms], major, True)
    else:
        total = terms[0]
        for d in range(1, n_major):
            moved = lax.ppermute(terms[d].astype(BF16), major, ring(n_major, -d))
            total = total + moved.astype(F32)
    pre_gate, pre_up = total[:, :LANES], total[:, LANES : 2 * LANES]
    back_hidden = total[:, 2 * LANES :] * scale
    sigma = jax.nn.sigmoid(pre_gate)
    activated = pre_gate * sigma
    slope = sigma * (1.0 + pre_gate * (1.0 - sigma))
    hidden = (activated * pre_up * scale).astype(BF16)
    grad_gate = (back_hidden * pre_up * slope).astype(BF16)
    grad_up = (back_hidden * activated).astype(BF16)
    terms = jnp.concatenate([hidden, grad_gate, grad_up], axis=1)
    if direct:
        gathered = gather_absolute(terms, major, True)
    else:
        gathered = [terms] + [
            lax.ppermute(terms, major, ring(n_major, d)) for d in range(1, n_major)
        ]
    hidden_all = jnp.concatenate([gathered[d][:, :LANES] for d in range(n_major)], axis=1)
    grads_all = jnp.concatenate([gathered[d][:, LANES:] for d in range(n_major)], axis=1)
    out = jnp.dot(hidden_all, w_back, preferred_element_type=F32).astype(BF16)
    grad = jnp.dot(grads_all, w_in, preferred_element_type=F32).astype(BF16)
    chunk = half // 2
    blocks = [
        jnp.concatenate(
            [out[:, j * chunk : (j + 1) * chunk], grad[:, j * chunk : (j + 1) * chunk]], axis=1
        )
        for j in range(n_minor)
    ]
    summed = sum_blocks(blocks, minor, direct)
    return summed.astype(BF16).reshape(n_z, ROWS, half)


def per_device(tokens, cotangent, route_devices, gate_fixed, w_gate, w_up, w_down):
    n_z, n_y, n_x = lax.axis_size("z"), lax.axis_size("y"), lax.axis_size("x")
    core, y, x = lax.axis_index("c"), lax.axis_index("y"), lax.axis_index("x")
    count, width = tokens.shape
    fanout = route_devices.shape[1]
    local_experts, units, _ = w_gate.shape
    group = local_experts * units
    quarter = width // n_y
    half = quarter // 2

    own = feature_part(tokens, cotangent, y, x, quarter)
    gate = (gate_fixed.astype(F32) / 65536.0).astype(BF16).T
    named = route_devices.T
    aux = jnp.concatenate([named.astype(BF16), gate], axis=0)
    aux = jnp.pad(aux, ((0, 16 - aux.shape[0]), (0, half - count)))
    lent = jnp.concatenate([feature_part(tokens, cotangent, x, y, quarter), aux], axis=0)
    other = lax.ppermute(lent, "c", [(0, 1), (1, 0)])
    other_aux = other[count:, :count]
    halves = [
        (own, *routing(named, gate, core, n_z)),
        (
            other[:count],
            *routing(
                other_aux[:fanout].astype(jnp.int32), other_aux[fanout : 3 * fanout], core, n_z
            ),
        ),
    ]

    def dispatch(part, onehot, gate_row):
        sent = jnp.dot(onehot, part, preferred_element_type=BF16).reshape(n_z, ROWS, half)
        last = jnp.pad(gate_row, ((0, 0), (0, half - gate_row.shape[1])))[:, None, :]
        is_last = lax.broadcasted_iota(jnp.int32, sent.shape, 1) == ROWS - 1
        return jnp.where(is_last, last, sent)

    sent = jnp.concatenate([dispatch(*h) for h in halves], axis=1)
    sent, w_gate, w_up, w_down = lax.optimization_barrier((sent, w_gate, w_up, w_down))
    arrived = lax.all_to_all(sent, "z", split_axis=0, concat_axis=0, tiled=True)

    kinds = jnp.concatenate([w.reshape(group, width) for w in (w_gate, w_up, w_down)], axis=0)
    by_y = exchange_weights(kinds, "y", n_y, group, quarter, True)
    by_x = exchange_weights(kinds, "x", n_x, group, quarter, False)
    arrived, by_y, by_x = lax.optimization_barrier((arrived, by_y, by_x))

    results = [
        experts(arrived[:, :ROWS], *by_y, "y", "x", units, True),
        experts(arrived[:, ROWS:], *by_x, "x", "y", units, False),
    ]
    returned = lax.all_to_all(
        jnp.concatenate(results, axis=1), "z", split_axis=0, concat_axis=0, tiled=True
    )

    def combine(onehot, rows):
        return lax.dot_general(
            onehot,
            rows.reshape(n_z * ROWS, half),
            (((0,), (0,)), ((), ())),
            preferred_element_type=F32,
        )

    theirs = combine(halves[1][1], returned[:, ROWS:]).astype(BF16)
    swap = [
        ((c * n_y + j) * n_x + i, ((1 - c) * n_y + i) * n_x + j)
        for c in range(2)
        for j in range(n_y)
        for i in range(n_x)
    ]
    theirs = lax.ppermute(theirs, ("c", "y", "x"), swap)
    result = (combine(halves[0][1], returned[:, :ROWS]) + theirs.astype(F32)).astype(BF16)
    return result[:, : half // 2], result[:, half // 2 :]


def solution(mesh):
    n_expert, n_tensor = mesh.devices.shape
    fine = Mesh(mesh.devices.reshape(n_expert // 2, 2, 4, n_tensor // 4), ("z", "c", "y", "x"))
    tokens = P(("z", "c"), None)
    weights = P(("z", "c"), ("y", "x"), None)
    outs = P(("z", "c"), ("y", "x"))
    return jax.shard_map(
        per_device,
        mesh=fine,
        in_specs=(tokens, tokens, tokens, tokens, weights, weights, weights),
        out_specs=(outs, outs),
        check_vma=False,
    )
```

```python
import functools

import jax
import jax.numpy as jnp
from jax import lax
from jax.experimental import pallas as pl
from jax.experimental.pallas import tpu as pltpu
from jax.sharding import Mesh
from jax.sharding import PartitionSpec as P

BF16 = jnp.bfloat16
F32 = jnp.float32
ROWS = 8
LANES = 128


def ring(size, step):
    return [(i, (i + step) % size) for i in range(size)]


def routing(named, gate, core, n_z):
    fanout, count = named.shape
    dests = 2 * lax.broadcasted_iota(jnp.int32, (n_z, count), 0) + core
    hits = [named[k][None, :] == dests for k in range(fanout)]
    member = hits[0]
    for hit in hits[1:]:
        member = member | hit
    earlier = (
        lax.broadcasted_iota(jnp.int32, (count, count), 0)
        < lax.broadcasted_iota(jnp.int32, (count, count), 1)
    ).astype(BF16)
    prior = jnp.dot(member.astype(BF16), earlier, preferred_element_type=F32).astype(jnp.int32)
    slot = jnp.where(member, prior, -1)
    chosen = slot[:, None, :] == lax.broadcasted_iota(jnp.int32, (n_z, ROWS, count), 1)
    gate_row = []
    for e in range(2):
        value = jnp.zeros((n_z, count), F32)
        for k in range(fanout):
            value = value + jnp.where(hits[k], gate[2 * k + e][None, :].astype(F32), 0.0)
        gate_row.append(jnp.sum(jnp.where(chosen, value[:, None, :], 0.0), axis=2))
    return (
        chosen.astype(BF16).reshape(n_z * ROWS, count),
        jnp.concatenate(gate_row, axis=1).astype(BF16),
    )


def exchange_weights(kinds, axis, n_groups, group, quarter, absolute):
    place = lax.axis_index(axis)
    w_in = jnp.zeros((n_groups, 2, LANES, quarter), BF16)
    w_back = jnp.zeros((n_groups, LANES, quarter), BF16)
    for d in range(n_groups):
        block = lax.dynamic_slice_in_dim(kinds, ((place + d) % n_groups) * quarter, quarter, 1)
        if d > 0:
            block = lax.ppermute(block, axis, ring(n_groups, d))
        block = block.reshape(3, group, quarter)
        at = (place - d) % n_groups if absolute else d
        w_in = lax.dynamic_update_slice(w_in, block[None, :2], (at, 0, 0, 0))
        w_back = lax.dynamic_update_slice(w_back, block[2:], (at, 0, 0))
    return (
        w_in.reshape(n_groups * 2 * LANES, quarter),
        w_back.reshape(n_groups * LANES, quarter),
    )


def feature_part(tokens, cotangent, major, minor, quarter):
    half = quarter // 2
    offset = quarter * major + half * (minor % 2)
    return jnp.where(
        minor < 2,
        lax.dynamic_slice_in_dim(tokens, offset, half, 1),
        lax.dynamic_slice_in_dim(cotangent, offset, half, 1),
    )


def gate_scale(received, units):
    n_z = received.shape[0]
    rows = n_z * ROWS
    owner = lax.broadcasted_iota(jnp.int32, (rows, n_z), 0) // ROWS
    spread = (owner == lax.broadcasted_iota(jnp.int32, (rows, n_z), 1)).astype(BF16)
    spread = jnp.dot(spread, received[:, ROWS - 1, :LANES], preferred_element_type=F32)
    lane = lax.broadcasted_iota(jnp.int32, (rows, LANES), 1)
    mine = lax.broadcasted_iota(jnp.int32, (rows, LANES), 0) % ROWS
    columns = [
        jnp.sum(jnp.where(lane == e * ROWS + mine, spread, 0.0), axis=1, keepdims=True)
        for e in range(2)
    ]
    return jnp.where(lane < units, columns[0], columns[1])


def local_call(kernel, outs, scratch, flops, args, scalars=0):
    specs = [pl.BlockSpec(memory_space=pltpu.SMEM)] * scalars
    specs += [pl.BlockSpec(memory_space=pltpu.VMEM)] * (len(args) - scalars)
    moved = sum(a.size * a.dtype.itemsize for a in args) + sum(o.size * 2 for o in outs)
    return pl.pallas_call(
        kernel,
        out_shape=outs,
        in_specs=specs,
        out_specs=[pl.BlockSpec(memory_space=pltpu.VMEM)] * len(outs),
        scratch_shapes=scratch,
        cost_estimate=pl.CostEstimate(flops=flops, bytes_accessed=moved, transcendentals=0),
        compiler_params=pltpu.CompilerParams(vmem_limit_bytes=16 * 1024 * 1024),
    )(*args)


def swap_blocks(blocks, axis):
    return lax.all_to_all(blocks, axis, split_axis=0, concat_axis=0, tiled=True)


def nt_dot(left, right):
    return lax.dot_general(left, right, (((1,), (1,)), ((), ())), preferred_element_type=F32)


def pre_kernel(size, direct, *refs):
    if direct:
        pieces, w_in, w_back, *outs = refs
        outs = [outs[0].at[g] for g in range(size)]
    else:
        place, *parts, w_in, w_back = refs[: size + 3]
        outs, pieces = refs[size + 3 : -1], refs[-1]
        for d in range(size):
            pieces[lax.rem(place[0] + size - d, size)] = parts[d][...]
    half = pieces.shape[2]
    for g in range(size):
        both = pl.ds(2 * LANES * g, 2 * LANES)
        one = pl.ds(LANES * g, LANES)
        pre = nt_dot(pieces[0], w_in[both, :half]) + nt_dot(pieces[1], w_in[both, half:])
        outs[g][:, : 2 * LANES] = pre.astype(BF16)
        back = nt_dot(pieces[2], w_back[one, :half]) + nt_dot(pieces[3], w_back[one, half:])
        outs[g][:, 2 * LANES :] = back.astype(BF16)


def hidden_kernel(size, direct, *refs):
    if direct:
        terms, scale, out = refs
        terms, outs = [terms.at[g] for g in range(size)], [out.at[g] for g in range(size)]
    else:
        terms, scale, outs = refs[:size], refs[size], refs[size + 1 :]
    total = [None] * 3
    for k in range(3):
        lanes = slice(LANES * k, LANES * (k + 1))
        for term in terms:
            value = term[:, lanes].astype(F32)
            total[k] = value if total[k] is None else total[k] + value
    pre_gate, pre_up, back = total
    gate = scale[...]
    back = back * gate
    sigma = 1.0 / (1.0 + jnp.exp(-pre_gate))
    activated = pre_gate * sigma
    slope = sigma * (1.0 + pre_gate * (1.0 - sigma))
    made = [activated * pre_up * gate, back * pre_up * slope, back * activated]
    for k in range(3):
        value = made[k].astype(BF16)
        for out in outs:
            out[:, LANES * k : LANES * (k + 1)] = value


def result_kernel(size, direct, *refs):
    hidden, grads, out_all, grad_all = refs[-4:]
    if direct:
        terms, w_in, w_back, made = refs[:-4]
        terms = [terms.at[g] for g in range(size)]
    else:
        place, *terms, w_in, w_back = refs[: size + 3]
        outs, made = refs[size + 3 : -5], refs[-5]
    for g in range(size):
        hidden[:, LANES * g : LANES * (g + 1)] = terms[g][:, :LANES]
        grads[:, 2 * LANES * g : 2 * LANES * (g + 1)] = terms[g][:, LANES:]
    quarter = w_in.shape[1]
    step = 2 * LANES
    for n in range(quarter // step):
        lanes = slice(n * step, (n + 1) * step)
        out_all[:, lanes] = jnp.dot(hidden[...], w_back[:, lanes], preferred_element_type=F32)
        grad_all[:, lanes] = jnp.dot(grads[...], w_in[:, lanes], preferred_element_type=F32)
    low = lax.broadcasted_iota(jnp.int32, (out_all.shape[0], LANES), 1) < LANES // 2
    tiles = quarter // LANES

    def plain(source, t):
        return source[:, LANES * t : LANES * (t + 1)]

    def moved(source, t):
        before = pltpu.roll(plain(source, (t + tiles - 1) % tiles), LANES // 2, 1)
        here = pltpu.roll(plain(source, t % tiles), LANES // 2, 1)
        return jnp.where(low, before, here)

    for j in range(size):
        if j % 2 == 0:
            t = 5 * j // 2
            row = [plain(out_all, t), plain(out_all, t + 1)]
            row.append(jnp.where(low, plain(out_all, t + 2), moved(grad_all, t)))
            row += [moved(grad_all, t + 1), moved(grad_all, t + 2)]
        else:
            t = (5 * j - 1) // 2
            row = [moved(out_all, t + 1), moved(out_all, t + 2)]
            row.append(jnp.where(low, moved(out_all, t + 3), plain(grad_all, t)))
            row += [plain(grad_all, t + 1), plain(grad_all, t + 2)]
        for k in range(5):
            made[j, :, LANES * k : LANES * (k + 1)] = row[k].astype(BF16)
    if not direct:
        for d in range(size):
            outs[d][...] = made[lax.rem(place[0] + d, size)]


def experts(direct_rows, other_rows, direct_weights, other_weights, units):
    size = lax.axis_size("x")
    n_z, _, half = direct_rows.shape
    rows, quarter = n_z * ROWS, 2 * half
    place = lax.axis_index("y").astype(jnp.int32)[None]
    flops = 6 * rows * quarter * LANES * size

    def shape(*dims):
        return jax.ShapeDtypeStruct(dims, BF16)

    def spread(value, axis):
        return [value] + [lax.ppermute(value, axis, ring(size, d)) for d in range(1, size)]

    def send(blocks, axis, sign):
        moved = [lax.ppermute(blocks[d], axis, ring(size, sign * d)) for d in range(1, size)]
        return [blocks[0], *moved]

    def in_step(ready, arrived):
        ready, arrived = lax.optimization_barrier((ready, tuple(arrived)))
        return ready, list(arrived)

    work = [
        pltpu.VMEM((rows, size * LANES), BF16),
        pltpu.VMEM((rows, 2 * size * LANES), BF16),
        pltpu.VMEM((rows, quarter), F32),
        pltpu.VMEM((rows, quarter), F32),
    ]
    stack = pltpu.VMEM((size, rows, half), BF16)
    wide = 3 * LANES

    flat = direct_rows.reshape(rows, half)
    pieces = swap_blocks(jnp.broadcast_to(flat[None], (size, rows, half)), "x")
    parts = spread(other_rows.reshape(rows, half), "y")
    direct_scale = gate_scale(direct_rows, units)
    other_scale = gate_scale(other_rows, units)

    pre = functools.partial(pre_kernel, size)
    (terms,) = local_call(
        functools.partial(pre, True), [shape(size, rows, wide)], [], flops, [pieces, *direct_weights]
    )
    terms, parts = in_step(terms, parts)
    terms = swap_blocks(terms, "y")
    partial = local_call(
        functools.partial(pre, False),
        [shape(rows, wide)] * size,
        [stack],
        flops,
        [place, *parts, *other_weights],
        1,
    )
    partial = send(partial, "x", -1)

    middle = functools.partial(hidden_kernel, size)
    (terms,) = local_call(
        functools.partial(middle, True), [shape(size, rows, wide)], [], 0, [terms, direct_scale]
    )
    terms, partial = in_step(terms, partial)
    terms = swap_blocks(terms, "y")
    (own,) = local_call(
        functools.partial(middle, False), [shape(rows, wide)], [], 0, [*partial, other_scale]
    )
    gathered = spread(own, "x")

    result = functools.partial(result_kernel, size)
    (blocks,) = local_call(
        functools.partial(result, True),
        [shape(size, rows, half)],
        work,
        flops,
        [terms, *direct_weights],
    )
    blocks, gathered = in_step(blocks, gathered)
    blocks = swap_blocks(blocks, "x")
    sums = local_call(
        functools.partial(result, False),
        [shape(rows, half)] * size,
        [stack, *work],
        flops,
        [place, *gathered, *other_weights],
        1,
    )
    sums = send(sums, "y", 1)
    first = jnp.sum(blocks.astype(F32), axis=0).astype(BF16)
    second = sum(b.astype(F32) for b in sums).astype(BF16)
    return [r.reshape(n_z, ROWS, half) for r in (first, second)]


def per_device(tokens, cotangent, route_devices, gate_fixed, w_gate, w_up, w_down):
    n_z, n_y, n_x = lax.axis_size("z"), lax.axis_size("y"), lax.axis_size("x")
    core, y, x = lax.axis_index("c"), lax.axis_index("y"), lax.axis_index("x")
    count, width = tokens.shape
    fanout = route_devices.shape[1]
    local_experts, units, _ = w_gate.shape
    group = local_experts * units
    quarter = width // n_y
    half = quarter // 2

    own = feature_part(tokens, cotangent, y, x, quarter)
    gate = (gate_fixed.astype(F32) / 65536.0).astype(BF16).T
    named = route_devices.T
    aux = jnp.concatenate([named.astype(BF16), gate], axis=0)
    aux = jnp.pad(aux, ((0, 16 - aux.shape[0]), (0, half - count)))
    lent = jnp.concatenate([feature_part(tokens, cotangent, x, y, quarter), aux], axis=0)
    other = lax.ppermute(lent, "c", [(0, 1), (1, 0)])
    other_aux = other[count:, :count]
    halves = [
        (own, *routing(named, gate, core, n_z)),
        (
            other[:count],
            *routing(
                other_aux[:fanout].astype(jnp.int32), other_aux[fanout : 3 * fanout], core, n_z
            ),
        ),
    ]

    def dispatch(part, onehot, gate_row):
        sent = jnp.dot(onehot, part, preferred_element_type=BF16).reshape(n_z, ROWS, half)
        last = jnp.pad(gate_row, ((0, 0), (0, half - gate_row.shape[1])))[:, None, :]
        is_last = lax.broadcasted_iota(jnp.int32, sent.shape, 1) == ROWS - 1
        return jnp.where(is_last, last, sent)

    sent = jnp.concatenate([dispatch(*h) for h in halves], axis=1)
    sent, w_gate, w_up, w_down = lax.optimization_barrier((sent, w_gate, w_up, w_down))
    arrived = lax.all_to_all(sent, "z", split_axis=0, concat_axis=0, tiled=True)

    kinds = jnp.concatenate([w.reshape(group, width) for w in (w_gate, w_up, w_down)], axis=0)
    by_y = exchange_weights(kinds, "y", n_y, group, quarter, True)
    by_x = exchange_weights(kinds, "x", n_x, group, quarter, False)
    arrived, by_y, by_x = lax.optimization_barrier((arrived, by_y, by_x))

    results = experts(arrived[:, :ROWS], arrived[:, ROWS:], by_y, by_x, units)
    returned = lax.all_to_all(
        jnp.concatenate(results, axis=1), "z", split_axis=0, concat_axis=0, tiled=True
    )

    def combine(onehot, rows):
        return lax.dot_general(
            onehot,
            rows.reshape(n_z * ROWS, half),
            (((0,), (0,)), ((), ())),
            preferred_element_type=F32,
        )

    theirs = combine(halves[1][1], returned[:, ROWS:]).astype(BF16)
    swap = [
        ((c * n_y + j) * n_x + i, ((1 - c) * n_y + i) * n_x + j)
        for c in range(2)
        for j in range(n_y)
        for i in range(n_x)
    ]
    theirs = lax.ppermute(theirs, ("c", "y", "x"), swap)
    result = (combine(halves[0][1], returned[:, :ROWS]) + theirs.astype(F32)).astype(BF16)
    return result[:, : half // 2], result[:, half // 2 :]


def solution(mesh):
    n_expert, n_tensor = mesh.devices.shape
    fine = Mesh(mesh.devices.reshape(n_expert // 2, 2, 4, n_tensor // 4), ("z", "c", "y", "x"))
    tokens = P(("z", "c"), None)
    weights = P(("z", "c"), ("y", "x"), None)
    outs = P(("z", "c"), ("y", "x"))
    return jax.shard_map(
        per_device,
        mesh=fine,
        in_specs=(tokens, tokens, tokens, tokens, weights, weights, weights),
        out_specs=(outs, outs),
        check_vma=False,
    )
```

```python
import functools

import jax
import jax.numpy as jnp
from jax import lax
from jax.experimental import pallas as pl
from jax.experimental.pallas import tpu as pltpu
from jax.sharding import Mesh
from jax.sharding import PartitionSpec as P

BF16 = jnp.bfloat16
F32 = jnp.float32
ROWS = 8
LANES = 128


def ring(size, step):
    return [(i, (i + step) % size) for i in range(size)]


def routing(named, gate, core, n_z):
    fanout, count = named.shape
    dests = 2 * lax.broadcasted_iota(jnp.int32, (n_z, count), 0) + core
    hits = [named[k][None, :] == dests for k in range(fanout)]
    member = hits[0]
    for hit in hits[1:]:
        member = member | hit
    earlier = (
        lax.broadcasted_iota(jnp.int32, (count, count), 0)
        < lax.broadcasted_iota(jnp.int32, (count, count), 1)
    ).astype(BF16)
    prior = jnp.dot(member.astype(BF16), earlier, preferred_element_type=F32).astype(jnp.int32)
    slot = jnp.where(member, prior, -1)
    chosen = slot[:, None, :] == lax.broadcasted_iota(jnp.int32, (n_z, ROWS, count), 1)
    gate_row = []
    for e in range(2):
        value = jnp.zeros((n_z, count), F32)
        for k in range(fanout):
            value = value + jnp.where(hits[k], gate[2 * k + e][None, :].astype(F32), 0.0)
        gate_row.append(jnp.sum(jnp.where(chosen, value[:, None, :], 0.0), axis=2))
    return (
        chosen.astype(BF16).reshape(n_z * ROWS, count),
        jnp.concatenate(gate_row, axis=1).astype(BF16),
    )


def exchange_weights(kinds, axis, n_groups, group, quarter, absolute):
    place = lax.axis_index(axis)
    w_in = jnp.zeros((n_groups, 2, LANES, quarter), BF16)
    w_back = jnp.zeros((n_groups, LANES, quarter), BF16)
    for d in range(n_groups):
        block = lax.dynamic_slice_in_dim(kinds, ((place + d) % n_groups) * quarter, quarter, 1)
        if d > 0:
            block = lax.ppermute(block, axis, ring(n_groups, d))
        block = block.reshape(3, group, quarter)
        at = (place - d) % n_groups if absolute else d
        w_in = lax.dynamic_update_slice(w_in, block[None, :2], (at, 0, 0, 0))
        w_back = lax.dynamic_update_slice(w_back, block[2:], (at, 0, 0))
    return (
        w_in.reshape(n_groups * 2 * LANES, quarter),
        w_back.reshape(n_groups * LANES, quarter),
    )


def feature_part(tokens, cotangent, major, minor, quarter):
    half = quarter // 2
    offset = quarter * major + half * (minor % 2)
    return jnp.where(
        minor < 2,
        lax.dynamic_slice_in_dim(tokens, offset, half, 1),
        lax.dynamic_slice_in_dim(cotangent, offset, half, 1),
    )


def gate_scale(gate_row, units):
    n_z = gate_row.shape[0]
    rows = n_z * ROWS
    owner = lax.broadcasted_iota(jnp.int32, (rows, n_z), 0) // ROWS
    spread = (owner == lax.broadcasted_iota(jnp.int32, (rows, n_z), 1)).astype(BF16)
    spread = jnp.dot(spread, gate_row, preferred_element_type=F32)
    lane = lax.broadcasted_iota(jnp.int32, (rows, LANES), 1)
    mine = lax.broadcasted_iota(jnp.int32, (rows, LANES), 0) % ROWS
    columns = [
        jnp.sum(jnp.where(lane == e * ROWS + mine, spread, 0.0), axis=1, keepdims=True)
        for e in range(2)
    ]
    return jnp.where(lane < units, columns[0], columns[1])


def whole(*dims):
    return pl.BlockSpec(dims, lambda g: (0,) * len(dims))


def leading(*dims):
    return pl.BlockSpec(dims, lambda g: (g,) + (0,) * (len(dims) - 1))


def local_call(kernel, steps, in_specs, out_specs, outs, scratch, flops, args):
    moved = sum(a.size * a.dtype.itemsize for a in args) + sum(o.size * 2 for o in outs)
    return pl.pallas_call(
        kernel,
        grid=(steps,),
        out_shape=outs,
        in_specs=in_specs,
        out_specs=out_specs,
        scratch_shapes=scratch,
        cost_estimate=pl.CostEstimate(flops=flops, bytes_accessed=moved, transcendentals=0),
        compiler_params=pltpu.CompilerParams(vmem_limit_bytes=60 * 1024 * 1024),
    )(*args)


def pack(first, second, gate_rows):
    n_z, _, half = first.shape
    chunks = half // LANES
    tiles = jnp.concatenate(
        [v.reshape(n_z, ROWS, chunks, LANES).swapaxes(1, 2) for v in (first, second)], axis=1
    )
    spare = jnp.concatenate([tiles[:, -1, : ROWS - 1], gate_rows], axis=1)
    tiles = tiles[:, :-1]
    is_last = lax.broadcasted_iota(jnp.int32, tiles.shape, 2) == ROWS - 1
    packed = jnp.where(is_last, spare[:, :, None, :], tiles)
    return packed.reshape(n_z, -1, LANES)


def unpack(packed):
    n_z = packed.shape[0]
    tiles = packed.reshape(n_z, -1, ROWS, LANES)
    chunks = (tiles.shape[1] + 1) // 2
    spare = tiles[:, :, ROWS - 1]
    last = jnp.pad(spare[:, : ROWS - 1], ((0, 0), (0, 1), (0, 0)))
    tiles = jnp.concatenate([tiles, last[:, None]], axis=1)
    halves = [
        t.swapaxes(1, 2).reshape(n_z, ROWS, chunks * LANES)
        for t in (tiles[:, :chunks], tiles[:, chunks:])
    ]
    return *halves, spare[:, ROWS - 1 :]


def swap_blocks(blocks, axis):
    return lax.all_to_all(blocks, axis, split_axis=0, concat_axis=0, tiled=True)


def nt_dot(left, right):
    return lax.dot_general(left, right, (((1,), (1,)), ((), ())), preferred_element_type=F32)


def pre_kernel(size, direct, *refs):
    g = pl.program_id(0)
    if direct:
        pieces, w_in, w_back, out = refs
        outs = [out.at[0]]
    else:
        place, *parts, w_in, w_back = refs[: size + 3]
        outs, pieces = refs[size + 3 : -1], refs[-1]

        @pl.when(g == 0)
        def _():
            for d in range(size):
                pieces[lax.rem(place[0] + size - d, size)] = parts[d][...]

    half = pieces.shape[2]
    pre = nt_dot(pieces[0], w_in[:, :half]) + nt_dot(pieces[1], w_in[:, half:])
    back = nt_dot(pieces[2], w_back[:, :half]) + nt_dot(pieces[3], w_back[:, half:])
    pre, back = pre.astype(BF16), back.astype(BF16)
    for d, out in enumerate(outs):

        @pl.when(direct or g == d)
        def _():
            out[:, : 2 * LANES] = pre
            out[:, 2 * LANES :] = back


def hidden_kernel(size, direct, *refs):
    if direct:
        terms, scale, out = refs
        terms, outs = [terms.at[g] for g in range(size)], [out.at[g] for g in range(size)]
    else:
        terms, scale, outs = refs[:size], refs[size], refs[size + 1 :]
    total = [None] * 3
    for k in range(3):
        lanes = slice(LANES * k, LANES * (k + 1))
        for term in terms:
            value = term[:, lanes].astype(F32)
            total[k] = value if total[k] is None else total[k] + value
    pre_gate, pre_up, back = total
    gate = scale[...]
    back = back * gate
    sigma = 1.0 / (1.0 + jnp.exp(-pre_gate))
    activated = pre_gate * sigma
    slope = sigma * (1.0 + pre_gate * (1.0 - sigma))
    made = [activated * pre_up * gate, back * pre_up * slope, back * activated]
    for k in range(3):
        value = made[k].astype(BF16)
        for out in outs:
            out[:, LANES * k : LANES * (k + 1)] = value


def result_kernel(size, direct, *refs):
    g = pl.program_id(0)
    out_all, grad_all = refs[-2:]
    if direct:
        terms, w_in, w_back, made = refs[:-2]
        term = terms[0]
    else:
        place, *terms, w_in, w_back = refs[: size + 3]
        outs, made = refs[size + 3 : -3], refs[-3]
        term = terms[0][...]
        for d in range(1, size):
            term = jnp.where(g == d, terms[d][...], term)
    out = jnp.dot(term[:, :LANES], w_back[...], preferred_element_type=F32)
    grad = jnp.dot(term[:, LANES:], w_in[...], preferred_element_type=F32)

    @pl.when(g == 0)
    def _():
        out_all[...] = out
        grad_all[...] = grad

    @pl.when(g > 0)
    def _():
        out_all[...] += out
        grad_all[...] += grad

    @pl.when(g == size - 1)
    def _():
        cut_blocks(size, out_all, grad_all, made)
        if not direct:
            for d in range(size):
                outs[d][...] = made[lax.rem(place[0] + d, size)]


def cut_blocks(size, out_all, grad_all, made):
    rows, quarter = out_all.shape
    low = lax.broadcasted_iota(jnp.int32, (rows, LANES), 1) < LANES // 2
    tiles = quarter // LANES

    def plain(source, t):
        return source[:, LANES * t : LANES * (t + 1)]

    def moved(source, t):
        before = pltpu.roll(plain(source, (t + tiles - 1) % tiles), LANES // 2, 1)
        here = pltpu.roll(plain(source, t % tiles), LANES // 2, 1)
        return jnp.where(low, before, here)

    for j in range(size):
        if j % 2 == 0:
            t = 5 * j // 2
            row = [plain(out_all, t), plain(out_all, t + 1)]
            row.append(jnp.where(low, plain(out_all, t + 2), moved(grad_all, t)))
            row += [moved(grad_all, t + 1), moved(grad_all, t + 2)]
        else:
            t = (5 * j - 1) // 2
            row = [moved(out_all, t + 1), moved(out_all, t + 2)]
            row.append(jnp.where(low, moved(out_all, t + 3), plain(grad_all, t)))
            row += [plain(grad_all, t + 1), plain(grad_all, t + 2)]
        for k in range(5):
            made[j, :, LANES * k : LANES * (k + 1)] = row[k].astype(BF16)


def experts(direct_rows, other_rows, gate_rows, direct_weights, other_weights, units):
    size = lax.axis_size("x")
    n_z, _, half = direct_rows.shape
    rows, quarter = n_z * ROWS, 2 * half
    place = lax.axis_index("y").astype(jnp.int32)[None]
    flops = 6 * rows * quarter * LANES * size

    def shape(*dims):
        return jax.ShapeDtypeStruct(dims, BF16)

    def spread(value, axis):
        return [value] + [lax.ppermute(value, axis, ring(size, d)) for d in range(1, size)]

    def send(blocks, axis, sign):
        moved = [lax.ppermute(blocks[d], axis, ring(size, sign * d)) for d in range(1, size)]
        return [blocks[0], *moved]

    def in_step(ready, arrived):
        ready, arrived = lax.optimization_barrier((ready, tuple(arrived)))
        return ready, list(arrived)

    wide = 3 * LANES
    tile = min(64, rows)
    sums_f32 = [pltpu.VMEM((rows, quarter), F32), pltpu.VMEM((rows, quarter), F32)]
    stack = pltpu.VMEM((size, rows, half), BF16)
    scalar = pl.BlockSpec(memory_space=pltpu.SMEM)
    weights = [leading(2 * LANES, quarter), leading(LANES, quarter)]
    pre = functools.partial(pre_kernel, size)
    middle = functools.partial(hidden_kernel, size)
    result = functools.partial(result_kernel, size)
    row_tile = leading(tile, wide)
    row_tiles = pl.BlockSpec((size, tile, wide), lambda i: (0, i, 0))

    flat = direct_rows.reshape(rows, half)
    pieces = swap_blocks(jnp.broadcast_to(flat[None], (size, rows, half)), "x")
    parts = spread(other_rows.reshape(rows, half), "y")
    direct_scale = gate_scale(gate_rows[:, 0], units)
    other_scale = gate_scale(gate_rows[:, 1], units)

    (terms,) = local_call(
        functools.partial(pre, True),
        size,
        [whole(size, rows, half), *weights],
        [leading(1, rows, wide)],
        [shape(size, rows, wide)],
        [],
        flops,
        [pieces, *direct_weights],
    )
    terms, parts = in_step(terms, parts)
    terms = swap_blocks(terms, "y")
    partial = local_call(
        functools.partial(pre, False),
        size,
        [scalar, *[whole(rows, half)] * size, *weights],
        [whole(rows, wide)] * size,
        [shape(rows, wide)] * size,
        [stack],
        flops,
        [place, *parts, *other_weights],
    )
    partial = send(partial, "x", -1)

    (terms,) = local_call(
        functools.partial(middle, True),
        rows // tile,
        [row_tiles, leading(tile, LANES)],
        [row_tiles],
        [shape(size, rows, wide)],
        [],
        0,
        [terms, direct_scale],
    )
    terms, partial = in_step(terms, partial)
    terms = swap_blocks(terms, "y")
    (own,) = local_call(
        functools.partial(middle, False),
        rows // tile,
        [*[row_tile] * size, leading(tile, LANES)],
        [row_tile],
        [shape(rows, wide)],
        [],
        0,
        [*partial, other_scale],
    )
    gathered = spread(own, "x")

    (blocks,) = local_call(
        functools.partial(result, True),
        size,
        [leading(1, rows, wide), *weights],
        [whole(size, rows, half)],
        [shape(size, rows, half)],
        sums_f32,
        flops,
        [terms, *direct_weights],
    )
    blocks, gathered = in_step(blocks, gathered)
    blocks = swap_blocks(blocks, "x")
    sums = local_call(
        functools.partial(result, False),
        size,
        [scalar, *[whole(rows, wide)] * size, *weights],
        [whole(rows, half)] * size,
        [shape(rows, half)] * size,
        [stack, *sums_f32],
        flops,
        [place, *gathered, *other_weights],
    )
    sums = send(sums, "y", 1)
    first = jnp.sum(blocks.astype(F32), axis=0).astype(BF16)
    second = sum(b.astype(F32) for b in sums).astype(BF16)
    return [r.reshape(n_z, ROWS, half) for r in (first, second)]


def per_device(tokens, cotangent, route_devices, gate_fixed, w_gate, w_up, w_down):
    n_z, n_y, n_x = lax.axis_size("z"), lax.axis_size("y"), lax.axis_size("x")
    core, y, x = lax.axis_index("c"), lax.axis_index("y"), lax.axis_index("x")
    count, width = tokens.shape
    fanout = route_devices.shape[1]
    local_experts, units, _ = w_gate.shape
    group = local_experts * units
    quarter = width // n_y
    half = quarter // 2

    own = feature_part(tokens, cotangent, y, x, quarter)
    gate = (gate_fixed.astype(F32) / 65536.0).astype(BF16).T
    named = route_devices.T
    aux = jnp.concatenate([named.astype(BF16), gate], axis=0)
    aux = jnp.pad(aux, ((0, 16 - aux.shape[0]), (0, half - count)))
    lent = jnp.concatenate([feature_part(tokens, cotangent, x, y, quarter), aux], axis=0)
    other = lax.ppermute(lent, "c", [(0, 1), (1, 0)])
    other_aux = other[count:, :count]
    halves = [
        (own, *routing(named, gate, core, n_z)),
        (
            other[:count],
            *routing(
                other_aux[:fanout].astype(jnp.int32), other_aux[fanout : 3 * fanout], core, n_z
            ),
        ),
    ]

    sent = [
        jnp.dot(onehot, part, preferred_element_type=BF16).reshape(n_z, ROWS, half)
        for part, onehot, _ in halves
    ]
    gate_rows = jnp.stack([gate_row for _, _, gate_row in halves], axis=1)
    gate_rows = jnp.pad(gate_rows, ((0, 0), (0, 0), (0, LANES - gate_rows.shape[2])))
    sent = pack(*sent, gate_rows)
    sent, w_gate, w_up, w_down = lax.optimization_barrier((sent, w_gate, w_up, w_down))
    arrived = lax.all_to_all(sent, "z", split_axis=0, concat_axis=0, tiled=True)

    kinds = jnp.concatenate([w.reshape(group, width) for w in (w_gate, w_up, w_down)], axis=0)
    by_y = exchange_weights(kinds, "y", n_y, group, quarter, True)
    by_x = exchange_weights(kinds, "x", n_x, group, quarter, False)
    arrived, by_y, by_x = lax.optimization_barrier((arrived, by_y, by_x))

    direct_rows, other_rows, gate_rows = unpack(arrived)
    results = experts(direct_rows, other_rows, gate_rows, by_y, by_x, units)
    returned = lax.all_to_all(
        pack(*results, jnp.zeros_like(gate_rows)), "z", split_axis=0, concat_axis=0, tiled=True
    )
    own_rows, other_rows, _ = unpack(returned)

    def combine(onehot, rows):
        return lax.dot_general(
            rows.reshape(n_z * ROWS, half),
            onehot,
            (((0,), (0,)), ((), ())),
            preferred_element_type=F32,
        )

    theirs = combine(halves[1][1], other_rows).astype(BF16)
    swap = [
        ((c * n_y + j) * n_x + i, ((1 - c) * n_y + i) * n_x + j)
        for c in range(2)
        for j in range(n_y)
        for i in range(n_x)
    ]
    theirs = lax.ppermute(theirs, ("c", "y", "x"), swap)
    result = (combine(halves[0][1], own_rows) + theirs.astype(F32)).astype(BF16)
    return result[: half // 2].T, result[half // 2 :].T


def solution(mesh):
    n_expert, n_tensor = mesh.devices.shape
    fine = Mesh(mesh.devices.reshape(n_expert // 2, 2, 4, n_tensor // 4), ("z", "c", "y", "x"))
    tokens = P(("z", "c"), None)
    weights = P(("z", "c"), ("y", "x"), None)
    outs = P(("z", "c"), ("y", "x"))
    return jax.shard_map(
        per_device,
        mesh=fine,
        in_specs=(tokens, tokens, tokens, tokens, weights, weights, weights),
        out_specs=(outs, outs),
        check_vma=False,
    )
```

```python
import functools

import jax
import jax.numpy as jnp
from jax import lax
from jax.experimental import pallas as pl
from jax.experimental.pallas import tpu as pltpu
from jax.sharding import Mesh
from jax.sharding import PartitionSpec as P

BF16 = jnp.bfloat16
F32 = jnp.float32
ROWS = 8
LANES = 128


def ring(size, step):
    return [(i, (i + step) % size) for i in range(size)]


def routing(named, gate, core, n_z):
    fanout, count = named.shape
    dests = 2 * lax.broadcasted_iota(jnp.int32, (n_z, count), 0) + core
    hits = [named[k][None, :] == dests for k in range(fanout)]
    member = hits[0]
    for hit in hits[1:]:
        member = member | hit
    earlier = (
        lax.broadcasted_iota(jnp.int32, (count, count), 0)
        < lax.broadcasted_iota(jnp.int32, (count, count), 1)
    ).astype(BF16)
    prior = jnp.dot(member.astype(BF16), earlier, preferred_element_type=F32).astype(jnp.int32)
    slot = jnp.where(member, prior, -1)
    chosen = slot[:, None, :] == lax.broadcasted_iota(jnp.int32, (n_z, ROWS, count), 1)
    gate_row = []
    for e in range(2):
        value = jnp.zeros((n_z, count), F32)
        for k in range(fanout):
            value = value + jnp.where(hits[k], gate[2 * k + e][None, :].astype(F32), 0.0)
        gate_row.append(jnp.sum(jnp.where(chosen, value[:, None, :], 0.0), axis=2))
    return (
        chosen.astype(BF16).reshape(n_z * ROWS, count),
        jnp.concatenate(gate_row, axis=1).astype(BF16),
    )


def exchange_weights(kinds, axis, n_groups, group, quarter, absolute):
    place = lax.axis_index(axis)
    w_in = jnp.zeros((n_groups, 2, LANES, quarter), BF16)
    w_back = jnp.zeros((n_groups, LANES, quarter), BF16)
    for d in range(n_groups):
        block = lax.dynamic_slice_in_dim(kinds, ((place + d) % n_groups) * quarter, quarter, 1)
        if d > 0:
            block = lax.ppermute(block, axis, ring(n_groups, d))
        block = block.reshape(3, group, quarter)
        at = (place - d) % n_groups if absolute else d
        w_in = lax.dynamic_update_slice(w_in, block[None, :2], (at, 0, 0, 0))
        w_back = lax.dynamic_update_slice(w_back, block[2:], (at, 0, 0))
    return (
        w_in.reshape(n_groups * 2 * LANES, quarter),
        w_back.reshape(n_groups * LANES, quarter),
    )


def feature_part(tokens, cotangent, major, minor, quarter):
    half = quarter // 2
    offset = quarter * major + half * (minor % 2)
    return jnp.where(
        minor < 2,
        lax.dynamic_slice_in_dim(tokens, offset, half, 1),
        lax.dynamic_slice_in_dim(cotangent, offset, half, 1),
    )


def gate_scale(gate_row, units):
    n_z = gate_row.shape[0]
    rows = n_z * ROWS
    owner = lax.broadcasted_iota(jnp.int32, (rows, n_z), 0) // ROWS
    spread = (owner == lax.broadcasted_iota(jnp.int32, (rows, n_z), 1)).astype(BF16)
    spread = jnp.dot(spread, gate_row, preferred_element_type=F32)
    lane = lax.broadcasted_iota(jnp.int32, (rows, LANES), 1)
    mine = lax.broadcasted_iota(jnp.int32, (rows, LANES), 0) % ROWS
    columns = [
        jnp.sum(jnp.where(lane == e * ROWS + mine, spread, 0.0), axis=1, keepdims=True)
        for e in range(2)
    ]
    return jnp.where(lane < units, columns[0], columns[1])


def local_call(kernel, outs, scratch, flops, args, scalars=0):
    specs = [pl.BlockSpec(memory_space=pltpu.SMEM)] * scalars
    specs += [pl.BlockSpec(memory_space=pltpu.VMEM)] * (len(args) - scalars)
    moved = sum(a.size * a.dtype.itemsize for a in args) + sum(o.size * 2 for o in outs)
    return pl.pallas_call(
        kernel,
        out_shape=outs,
        in_specs=specs,
        out_specs=[pl.BlockSpec(memory_space=pltpu.VMEM)] * len(outs),
        scratch_shapes=scratch,
        cost_estimate=pl.CostEstimate(flops=flops, bytes_accessed=moved, transcendentals=0),
        compiler_params=pltpu.CompilerParams(vmem_limit_bytes=60 * 1024 * 1024),
    )(*args)


def pack(first, second, gate_rows):
    n_z, _, half = first.shape
    chunks = half // LANES
    tiles = jnp.concatenate(
        [v.reshape(n_z, ROWS, chunks, LANES).swapaxes(1, 2) for v in (first, second)], axis=1
    )
    spare = jnp.concatenate([tiles[:, -1, : ROWS - 1], gate_rows], axis=1)
    tiles = tiles[:, :-1]
    is_last = lax.broadcasted_iota(jnp.int32, tiles.shape, 2) == ROWS - 1
    packed = jnp.where(is_last, spare[:, :, None, :], tiles)
    return packed.reshape(n_z, -1, LANES)


def unpack(packed):
    n_z = packed.shape[0]
    tiles = packed.reshape(n_z, -1, ROWS, LANES)
    chunks = (tiles.shape[1] + 1) // 2
    spare = tiles[:, :, ROWS - 1]
    last = jnp.pad(spare[:, : ROWS - 1], ((0, 0), (0, 1), (0, 0)))
    tiles = jnp.concatenate([tiles, last[:, None]], axis=1)
    halves = [
        t.swapaxes(1, 2).reshape(n_z, ROWS, chunks * LANES)
        for t in (tiles[:, :chunks], tiles[:, chunks:])
    ]
    return *halves, spare[:, ROWS - 1 :]


def swap_blocks(blocks, axis):
    return lax.all_to_all(blocks, axis, split_axis=0, concat_axis=0, tiled=True)


def nt_dot(left, right):
    return lax.dot_general(left, right, (((1,), (1,)), ((), ())), preferred_element_type=F32)


def pre_kernel(size, direct, *refs):
    if direct:
        pieces, w_in, w_back, *outs = refs
        outs = [outs[0].at[g] for g in range(size)]
    else:
        place, *parts, w_in, w_back = refs[: size + 3]
        outs, pieces = refs[size + 3 : -1], refs[-1]
        for d in range(size):
            pieces[lax.rem(place[0] + size - d, size)] = parts[d][...]
    half = pieces.shape[2]
    for g in range(size):
        both = pl.ds(2 * LANES * g, 2 * LANES)
        one = pl.ds(LANES * g, LANES)
        pre = nt_dot(pieces[0], w_in[both, :half]) + nt_dot(pieces[1], w_in[both, half:])
        outs[g][:, : 2 * LANES] = pre.astype(BF16)
        back = nt_dot(pieces[2], w_back[one, :half]) + nt_dot(pieces[3], w_back[one, half:])
        outs[g][:, 2 * LANES :] = back.astype(BF16)


def hidden_kernel(size, direct, *refs):
    if direct:
        terms, scale, out = refs
        terms, outs = [terms.at[g] for g in range(size)], [out.at[g] for g in range(size)]
    else:
        terms, scale, outs = refs[:size], refs[size], refs[size + 1 :]
    total = [None] * 3
    for k in range(3):
        lanes = slice(LANES * k, LANES * (k + 1))
        for term in terms:
            value = term[:, lanes].astype(F32)
            total[k] = value if total[k] is None else total[k] + value
    pre_gate, pre_up, back = total
    gate = scale[...]
    back = back * gate
    sigma = 1.0 / (1.0 + jnp.exp(-pre_gate))
    activated = pre_gate * sigma
    slope = sigma * (1.0 + pre_gate * (1.0 - sigma))
    made = [activated * pre_up * gate, back * pre_up * slope, back * activated]
    for k in range(3):
        value = made[k].astype(BF16)
        for out in outs:
            out[:, LANES * k : LANES * (k + 1)] = value


def result_kernel(size, direct, *refs):
    hidden, grads, out_all, grad_all = refs[-4:]
    if direct:
        terms, w_in, w_back, made = refs[:-4]
        terms = [terms.at[g] for g in range(size)]
    else:
        place, *terms, w_in, w_back = refs[: size + 3]
        outs, made = refs[size + 3 : -5], refs[-5]
    for g in range(size):
        hidden[:, LANES * g : LANES * (g + 1)] = terms[g][:, :LANES]
        grads[:, 2 * LANES * g : 2 * LANES * (g + 1)] = terms[g][:, LANES:]
    quarter = w_in.shape[1]
    step = 2 * LANES
    for n in range(quarter // step):
        lanes = slice(n * step, (n + 1) * step)
        out_all[:, lanes] = jnp.dot(hidden[...], w_back[:, lanes], preferred_element_type=F32)
        grad_all[:, lanes] = jnp.dot(grads[...], w_in[:, lanes], preferred_element_type=F32)
    low = lax.broadcasted_iota(jnp.int32, (out_all.shape[0], LANES), 1) < LANES // 2
    tiles = quarter // LANES

    def plain(source, t):
        return source[:, LANES * t : LANES * (t + 1)]

    def moved(source, t):
        before = pltpu.roll(plain(source, (t + tiles - 1) % tiles), LANES // 2, 1)
        here = pltpu.roll(plain(source, t % tiles), LANES // 2, 1)
        return jnp.where(low, before, here)

    for j in range(size):
        if j % 2 == 0:
            t = 5 * j // 2
            row = [plain(out_all, t), plain(out_all, t + 1)]
            row.append(jnp.where(low, plain(out_all, t + 2), moved(grad_all, t)))
            row += [moved(grad_all, t + 1), moved(grad_all, t + 2)]
        else:
            t = (5 * j - 1) // 2
            row = [moved(out_all, t + 1), moved(out_all, t + 2)]
            row.append(jnp.where(low, moved(out_all, t + 3), plain(grad_all, t)))
            row += [plain(grad_all, t + 1), plain(grad_all, t + 2)]
        for k in range(5):
            made[j, :, LANES * k : LANES * (k + 1)] = row[k].astype(BF16)
    if not direct:
        for d in range(size):
            outs[d][...] = made[lax.rem(place[0] + d, size)]


def experts(direct_rows, other_rows, gate_rows, direct_weights, other_weights, units):
    size = lax.axis_size("x")
    n_z, _, half = direct_rows.shape
    rows, quarter = n_z * ROWS, 2 * half
    place = lax.axis_index("y").astype(jnp.int32)[None]
    flops = 6 * rows * quarter * LANES * size

    def shape(*dims):
        return jax.ShapeDtypeStruct(dims, BF16)

    def spread(value, axis):
        return [value] + [lax.ppermute(value, axis, ring(size, d)) for d in range(1, size)]

    def send(blocks, axis, sign):
        moved = [lax.ppermute(blocks[d], axis, ring(size, sign * d)) for d in range(1, size)]
        return [blocks[0], *moved]

    def in_step(ready, arrived):
        ready, arrived = lax.optimization_barrier((ready, tuple(arrived)))
        return ready, list(arrived)

    work = [
        pltpu.VMEM((rows, size * LANES), BF16),
        pltpu.VMEM((rows, 2 * size * LANES), BF16),
        pltpu.VMEM((rows, quarter), F32),
        pltpu.VMEM((rows, quarter), F32),
    ]
    stack = pltpu.VMEM((size, rows, half), BF16)
    wide = 3 * LANES

    flat = direct_rows.reshape(rows, half)
    pieces = swap_blocks(jnp.broadcast_to(flat[None], (size, rows, half)), "x")
    parts = spread(other_rows.reshape(rows, half), "y")
    direct_scale = gate_scale(gate_rows[:, 0], units)
    other_scale = gate_scale(gate_rows[:, 1], units)

    pre = functools.partial(pre_kernel, size)
    (terms,) = local_call(
        functools.partial(pre, True), [shape(size, rows, wide)], [], flops, [pieces, *direct_weights]
    )
    terms, parts = in_step(terms, parts)
    terms = swap_blocks(terms, "y")
    partial = local_call(
        functools.partial(pre, False),
        [shape(rows, wide)] * size,
        [stack],
        flops,
        [place, *parts, *other_weights],
        1,
    )
    partial = send(partial, "x", -1)

    middle = functools.partial(hidden_kernel, size)
    (terms,) = local_call(
        functools.partial(middle, True), [shape(size, rows, wide)], [], 0, [terms, direct_scale]
    )
    terms, partial = in_step(terms, partial)
    terms = swap_blocks(terms, "y")
    (own,) = local_call(
        functools.partial(middle, False), [shape(rows, wide)], [], 0, [*partial, other_scale]
    )
    gathered = spread(own, "x")

    result = functools.partial(result_kernel, size)
    (blocks,) = local_call(
        functools.partial(result, True),
        [shape(size, rows, half)],
        work,
        flops,
        [terms, *direct_weights],
    )
    blocks, gathered = in_step(blocks, gathered)
    blocks = swap_blocks(blocks, "x")
    sums = local_call(
        functools.partial(result, False),
        [shape(rows, half)] * size,
        [stack, *work],
        flops,
        [place, *gathered, *other_weights],
        1,
    )
    sums = send(sums, "y", 1)
    first = jnp.sum(blocks.astype(F32), axis=0).astype(BF16)
    second = sum(b.astype(F32) for b in sums).astype(BF16)
    return [r.reshape(n_z, ROWS, half) for r in (first, second)]


def per_device(tokens, cotangent, route_devices, gate_fixed, w_gate, w_up, w_down):
    n_z, n_y, n_x = lax.axis_size("z"), lax.axis_size("y"), lax.axis_size("x")
    core, y, x = lax.axis_index("c"), lax.axis_index("y"), lax.axis_index("x")
    count, width = tokens.shape
    fanout = route_devices.shape[1]
    local_experts, units, _ = w_gate.shape
    group = local_experts * units
    quarter = width // n_y
    half = quarter // 2

    own = feature_part(tokens, cotangent, y, x, quarter)
    gate = (gate_fixed.astype(F32) / 65536.0).astype(BF16).T
    named = route_devices.T
    aux = jnp.concatenate([named.astype(BF16), gate], axis=0)
    aux = jnp.pad(aux, ((0, 16 - aux.shape[0]), (0, half - count)))
    lent = jnp.concatenate([feature_part(tokens, cotangent, x, y, quarter), aux], axis=0)
    other = lax.ppermute(lent, "c", [(0, 1), (1, 0)])
    other_aux = other[count:, :count]
    halves = [
        (own, *routing(named, gate, core, n_z)),
        (
            other[:count],
            *routing(
                other_aux[:fanout].astype(jnp.int32), other_aux[fanout : 3 * fanout], core, n_z
            ),
        ),
    ]

    sent = [
        jnp.dot(onehot, part, preferred_element_type=BF16).reshape(n_z, ROWS, half)
        for part, onehot, _ in halves
    ]
    gate_rows = jnp.stack([gate_row for _, _, gate_row in halves], axis=1)
    gate_rows = jnp.pad(gate_rows, ((0, 0), (0, 0), (0, LANES - gate_rows.shape[2])))
    sent = pack(*sent, gate_rows)
    sent, w_gate, w_up, w_down = lax.optimization_barrier((sent, w_gate, w_up, w_down))
    arrived = lax.all_to_all(sent, "z", split_axis=0, concat_axis=0, tiled=True)

    kinds = jnp.concatenate([w.reshape(group, width) for w in (w_gate, w_up, w_down)], axis=0)
    by_y = exchange_weights(kinds, "y", n_y, group, quarter, True)
    by_x = exchange_weights(kinds, "x", n_x, group, quarter, False)
    arrived, by_y, by_x = lax.optimization_barrier((arrived, by_y, by_x))

    direct_rows, other_rows, gate_rows = unpack(arrived)
    results = experts(direct_rows, other_rows, gate_rows, by_y, by_x, units)
    returned = lax.all_to_all(
        pack(*results, jnp.zeros_like(gate_rows)), "z", split_axis=0, concat_axis=0, tiled=True
    )
    own_rows, other_rows, _ = unpack(returned)

    def combine(onehot, rows):
        return lax.dot_general(
            rows.reshape(n_z * ROWS, half),
            onehot,
            (((0,), (0,)), ((), ())),
            preferred_element_type=F32,
        )

    theirs = combine(halves[1][1], other_rows).astype(BF16)
    swap = [
        ((c * n_y + j) * n_x + i, ((1 - c) * n_y + i) * n_x + j)
        for c in range(2)
        for j in range(n_y)
        for i in range(n_x)
    ]
    theirs = lax.ppermute(theirs, ("c", "y", "x"), swap)
    result = (combine(halves[0][1], own_rows) + theirs.astype(F32)).astype(BF16)
    return result[: half // 2].T, result[half // 2 :].T


def solution(mesh):
    n_expert, n_tensor = mesh.devices.shape
    fine = Mesh(mesh.devices.reshape(n_expert // 2, 2, 4, n_tensor // 4), ("z", "c", "y", "x"))
    tokens = P(("z", "c"), None)
    weights = P(("z", "c"), ("y", "x"), None)
    outs = P(("z", "c"), ("y", "x"))
    return jax.shard_map(
        per_device,
        mesh=fine,
        in_specs=(tokens, tokens, tokens, tokens, weights, weights, weights),
        out_specs=(outs, outs),
        check_vma=False,
    )
```
